32 devices in a mesh: op: 8 (over y, x, core), sec: 4 (over z).
Axes of the slice: x: 2, y: 2, z: 4, core: 2. Of those that a mesh axis runs over, the one named last changes fastest.
Arguments:
- wave: bfloat16 [32, 256, 4, 256], P('op'), may hold values from -6 to 6
- sector_dims: int32 [32], replicated, may hold values from 64 to 256, as said below
- left_ops: bfloat16 [32, 32, 256, 256], P(None, ('op', 'sec')), may hold values from -0.375 to 0.375
- right_ops: bfloat16 [32, 8, 4, 256, 256], P('op', None, 'sec'), may hold values from -0.375 to 0.375
- site_ops: float32 [32, 4, 4], replicated, may hold values from -0.5 to 0.5
Outputs:
- sigma: bfloat16 [32, 256, 4, 256], P('op', 'sec')
The draws below stay inside these ranges and needn't reach their ends.
Inputs may be any that keep to these rules, and one draw needn't show every extreme that they name: `sector_dims`: every entry is a multiple of 64, and at least one sector has exactly 256 states.
All inputs are finite; a program needn't handle non-finite values.
Results may differ from the reference program's by a relative error of at most 0.005.
Values may be sent and summed in bfloat16 or wider, within the bound.
A program may use at most 128 MiB of HBM per device.

```python
import jax
import jax.numpy as jnp
from jax import lax

SECTORS = 32
BM = 256
GRAIN = 64
P_SIZE = 4
TERM_DEV = 1
TERMS = 32
N_OP = 8
N_SEC = 4


def draw_sector_dims(key, part):
    first_key, second_key = jax.random.split(key)
    counts = jax.random.randint(first_key, (SECTORS,), 1, BM // GRAIN + 1)
    chosen = jax.random.randint(second_key, (), 0, SECTORS)
    places = jnp.arange(SECTORS, dtype=jnp.int32)
    return jnp.where(places == chosen, BM, counts * GRAIN).astype(jnp.int32)


def level_of(key, dims, shards, low, top_value):
    level, own = 1.0, jax.random.fold_in(key, 6)
    for axis_at, blocks in shards:
        heights = jnp.exp(jax.random.uniform(jax.random.fold_in(own, axis_at), (blocks,), jnp.float32, low / len(shards), top_value / len(shards)))
        level = level * jnp.repeat(heights, dims[axis_at] // blocks).reshape([-1 if axis == axis_at else 1 for axis in range(len(dims))])
    return level


def normal_values(key, dims, width, limit, shards=(), kind=jnp.bfloat16):
    entries = width * jax.random.normal(key, dims, jnp.float32)
    if shards:
        entries = entries * level_of(key, dims, shards, -0.22, 0.18)
    return jnp.clip(entries, -limit, limit).astype(kind)


def setup_inputs(seed: int = 0) -> dict:
    streams_of = jax.random.split(jax.random.key(seed), 6)
    wave = normal_values(streams_of[0], (SECTORS, BM, P_SIZE, BM), 1.0, 6.0, ((0, 8),))
    sector_dims = draw_sector_dims(jax.random.fold_in(streams_of[5], 71), 0)
    left_ops = normal_values(streams_of[2], (SECTORS, TERMS, BM, BM), BM ** -0.5, 0.375, ((1, 32),))
    right_ops = normal_values(streams_of[3], (SECTORS, N_OP, N_SEC * TERM_DEV, BM, BM), BM ** -0.5, 0.375, ((0, 8), (2, 4)))
    site_ops = normal_values(streams_of[4], (TERMS, P_SIZE, P_SIZE), (P_SIZE * TERMS) ** -0.5, 0.5, (), jnp.float32)
    return {"wave": wave, "sector_dims": sector_dims, "left_ops": left_ops, "right_ops": right_ops, "site_ops": site_ops}


def reference(wave, sector_dims, left_ops, right_ops, site_ops):
    positions = jnp.arange(BM, dtype=jnp.int32)
    mask = (positions[None, :] < sector_dims[:, None]).astype(jnp.float32)
    masked = (wave.astype(jnp.float32) * mask[:, :, None, None] * mask[:, None, None, :]).astype(jnp.bfloat16)
    masked_wide = masked.astype(jnp.float32)
    right_all = right_ops.reshape(SECTORS, TERMS, BM, BM)

    def add_term(total, inputs):
        left_block, right_block, site_mat = inputs
        first = jnp.einsum('slm,smpr->slpr', left_block.astype(jnp.float32), masked_wide)
        second = jnp.einsum('slpr,qp->slqr', first, site_mat, precision=lax.Precision.HIGHEST)
        inter = second.astype(jnp.bfloat16)
        contrib = jnp.einsum('slqm,srm->slqr', inter.astype(jnp.float32), right_block.astype(jnp.float32))
        return total + contrib, None

    start = jnp.zeros((SECTORS, BM, P_SIZE, BM), jnp.float32)
    total, _ = lax.scan(add_term, start, (jnp.swapaxes(left_ops, 0, 1), jnp.swapaxes(right_all, 0, 1), site_ops))
    return (total * mask[:, :, None, None] * mask[:, None, None, :]).astype(jnp.bfloat16)
```

```python
import functools

import jax
import jax.numpy as jnp
from jax import lax
from jax.experimental import pallas as pl
from jax.experimental.pallas import tpu as pltpu
from jax.sharding import PartitionSpec as P

MESH = pl.DeviceIdType.MESH
MIB = 1024 * 1024


def sector_mask(sizes, width):
    places = lax.broadcasted_iota(jnp.int32, (sizes.shape[0], width), 1)
    return (places < sizes[:, None]).astype(jnp.float32)


def kernel(
    n_op, n_sec, site_ref, psi_hbm, left_hbm, right_hbm, out_ref,
    psi, right, left, mixed, total, zsend, zrecv,
    psi_sem, right_sem, own_sem, lsend_sem, lrecv_sem, zsend_sem, zrecv_sem,
):
    o = lax.axis_index("op")
    z = lax.axis_index("sec")
    sectors, p_size, width = psi.shape[0], psi.shape[1], psi.shape[2]
    rows = width // n_sec
    chunk = width // 4

    def psi_copy(j):
        return pltpu.make_async_copy(psi_hbm.at[j], psi.at[j], psi_sem.at[j])

    def right_copy(j):
        return pltpu.make_async_copy(right_hbm.at[j], right.at[j], right_sem.at[j])

    def own_copy(j):
        return pltpu.make_async_copy(left_hbm.at[o, j], left.at[j, o], own_sem.at[j])

    def left_out(j, peer):
        return pltpu.make_async_remote_copy(
            src_ref=left_hbm.at[peer, j], dst_ref=left.at[j, o],
            send_sem=lsend_sem.at[j, peer], recv_sem=lrecv_sem.at[j, o],
            device_id=(peer, z), device_id_type=MESH,
        )

    def left_in(j, peer):
        return pltpu.make_async_remote_copy(
            src_ref=left_hbm.at[peer, j], dst_ref=left.at[j, peer],
            send_sem=lsend_sem.at[j, peer], recv_sem=lrecv_sem.at[j, peer],
            device_id=(peer, z), device_id_type=MESH,
        )

    def part_out(j, peer):
        return pltpu.make_async_remote_copy(
            src_ref=zsend.at[j, pl.ds(pl.multiple_of(peer * rows, rows), rows)],
            dst_ref=zrecv.at[j, z],
            send_sem=zsend_sem.at[j, peer], recv_sem=zrecv_sem.at[j, z],
            device_id=(o, peer), device_id_type=MESH,
        )

    def part_in(j, peer):
        return pltpu.make_async_remote_copy(
            src_ref=zsend.at[j, pl.ds(pl.multiple_of(peer * rows, rows), rows)],
            dst_ref=zrecv.at[j, peer],
            send_sem=zsend_sem.at[j, peer], recv_sem=zrecv_sem.at[j, peer],
            device_id=(o, peer), device_id_type=MESH,
        )

    def op_peers(body):
        def step(i, _):
            body(lax.rem(o + i, n_op))
            return 0
        lax.fori_loop(1, n_op, step, 0)

    def sec_peers(body):
        def step(i, _):
            body(lax.rem(z + i, n_sec))
            return 0
        lax.fori_loop(1, n_sec, step, 0)

    barrier = pltpu.get_barrier_semaphore()
    op_peers(lambda peer: pl.semaphore_signal(
        barrier, inc=1, device_id=(peer, z), device_id_type=MESH))
    sec_peers(lambda peer: pl.semaphore_signal(
        barrier, inc=1, device_id=(o, peer), device_id_type=MESH))
    for j in range(sectors):
        psi_copy(j).start()
        right_copy(j).start()
        own_copy(j).start()
    pl.semaphore_wait(barrier, n_op + n_sec - 2)

    for j in range(sectors):
        op_peers(lambda peer: left_out(j, peer).start())

    def mix(j):
        psi_copy(j).wait()
        right_copy(j).wait()

        def one_term(a, _):
            block = right[j, a]
            term = a * n_sec + z
            weights = [[site_ref[term, q, p] for p in range(p_size)] for q in range(p_size)]
            for c in range(width // chunk):
                here = pl.ds(c * chunk, chunk)
                waves = psi[j, :, here, :].reshape(p_size * chunk, width)
                got = lax.dot_general(
                    waves, block, (((1,), (1,)), ((), ())), preferred_element_type=jnp.float32
                )
                for q in range(p_size):
                    value = weights[q][0] * got[:chunk]
                    for p in range(1, p_size):
                        value = value + weights[q][p] * got[p * chunk:(p + 1) * chunk]
                    mixed[j, a, here, pl.ds(q * width, width)] = value.astype(jnp.bfloat16)
            return 0

        lax.fori_loop(0, n_op, one_term, 0)

    def contract(j):
        own_copy(j).wait()
        op_peers(lambda peer: left_in(j, peer).wait_recv())

        def one_state(q, _):
            cols = pl.ds(pl.multiple_of(q * width, width), width)
            value = jnp.dot(left[j, 0], mixed[j, 0, :, cols], preferred_element_type=jnp.float32)
            for a in range(1, n_op):
                value = value + jnp.dot(
                    left[j, a], mixed[j, a, :, cols], preferred_element_type=jnp.float32
                )
            total[j, :, cols] = value
            zsend[j, :, cols] = value.astype(jnp.bfloat16)
            return 0

        lax.fori_loop(0, p_size, one_state, 0)
        sec_peers(lambda peer: part_out(j, peer).start())

    mix(0)
    for j in range(sectors):
        if j + 1 < sectors:
            mix(j + 1)
        contract(j)

    for j in range(sectors):
        sec_peers(lambda peer: part_in(j, peer).wait_recv())
        value = total[j, pl.ds(pl.multiple_of(z * rows, rows), rows), :]
        for i in range(1, n_sec):
            value = value + zrecv[j, lax.rem(z + i, n_sec)].astype(jnp.float32)
        out_ref[j] = value.astype(jnp.bfloat16)

    for j in range(sectors):
        op_peers(lambda peer: left_out(j, peer).wait_send())
        sec_peers(lambda peer: part_out(j, peer).wait_send())


def shards(wave, sector_dims, left_ops, right_ops, site_ops):
    n_op = lax.axis_size("op")
    n_sec = lax.axis_size("sec")
    o = lax.axis_index("op")
    z = lax.axis_index("sec")
    sectors, width, p_size = wave.shape[0], wave.shape[1], wave.shape[2]
    rows = width // n_sec
    own_sizes = lax.dynamic_slice_in_dim(sector_dims, o * sectors, sectors)
    own_mask = sector_mask(own_sizes, width)
    masked = (
        wave.astype(jnp.float32) * own_mask[:, :, None, None] * own_mask[:, None, None, :]
    ).astype(jnp.bfloat16)
    masked = jnp.transpose(masked, (0, 2, 1, 3))
    left = left_ops.reshape(n_op, sectors, width, width)
    right = right_ops.reshape(sectors, n_op, width, width)
    wide = p_size * width
    flops = 4 * sectors * n_op * width * width * wide
    partial = pl.pallas_call(
        functools.partial(kernel, n_op, n_sec),
        out_shape=jax.ShapeDtypeStruct((sectors, rows, wide), jnp.bfloat16),
        in_specs=[
            pl.BlockSpec(memory_space=pltpu.SMEM),
            pl.BlockSpec(memory_space=pl.ANY),
            pl.BlockSpec(memory_space=pl.ANY),
            pl.BlockSpec(memory_space=pl.ANY),
        ],
        out_specs=pl.BlockSpec(memory_space=pltpu.VMEM),
        scratch_shapes=[
            pltpu.VMEM((sectors, p_size, width, width), jnp.bfloat16),
            pltpu.VMEM((sectors, n_op, width, width), jnp.bfloat16),
            pltpu.VMEM((sectors, n_op, width, width), jnp.bfloat16),
            pltpu.VMEM((sectors, n_op, width, wide), jnp.bfloat16),
            pltpu.VMEM((sectors, width, wide), jnp.float32),
            pltpu.VMEM((sectors, width, wide), jnp.bfloat16),
            pltpu.VMEM((sectors, n_sec, rows, wide), jnp.bfloat16),
            pltpu.SemaphoreType.DMA((sectors,)),
            pltpu.SemaphoreType.DMA((sectors,)),
            pltpu.SemaphoreType.DMA((sectors,)),
            pltpu.SemaphoreType.DMA((sectors, n_op)),
            pltpu.SemaphoreType.DMA((sectors, n_op)),
            pltpu.SemaphoreType.DMA((sectors, n_sec)),
            pltpu.SemaphoreType.DMA((sectors, n_sec)),
        ],
        compiler_params=pltpu.CompilerParams(
            collective_id=0, has_side_effects=True, vmem_limit_bytes=48 * MIB
        ),
        cost_estimate=pl.CostEstimate(flops=flops, bytes_accessed=12 * MIB, transcendentals=0),
    )(site_ops, masked, left, right)
    row_mask = lax.dynamic_slice_in_dim(own_mask, z * rows, rows, 1)
    sigma = partial.reshape(sectors, rows, p_size, width).astype(jnp.float32)
    return (sigma * row_mask[:, :, None, None] * own_mask[:, None, None, :]).astype(jnp.bfloat16)


def solution(mesh):
    placed = (
        P("op", None, None, None),
        P(),
        P(None, ("op", "sec"), None, None),
        P("op", None, "sec", None, None),
        P(),
    )
    return jax.shard_map(
        shards, mesh=mesh, in_specs=placed, out_specs=P("op", "sec", None, None), check_vma=False
    )
```

```python
import functools

import jax
import jax.numpy as jnp
from jax import lax
from jax.experimental import pallas as pl
from jax.experimental.pallas import tpu as pltpu
from jax.sharding import PartitionSpec as P

MESH = pl.DeviceIdType.MESH
MIB = 1024 * 1024


def kernel(
    n_op, n_sec, site_ref, dims_ref, psi_hbm, left_hbm, right_hbm, out_ref,
    psi, right, left, mixed, total, zsend, zrecv, relayed,
    psi_sem, right_sem, own_sem, lsend_sem, lrecv_sem, zsend_sem, zrecv_sem, relay_sem,
):
    o = lax.axis_index("op")
    z = lax.axis_index("sec")
    sectors, p_size, width = psi.shape[0], psi.shape[1], psi.shape[2]
    rows = width // n_sec
    chunk = width // 4
    relays = n_sec == 4

    if relays:
        half = z // 2
        beside = z + 1 - 2 * lax.rem(z, 2)
        far = 3 * (1 - half)
        order = [far, 2 - half, beside, z]
        outer = lax.rem(z, 3) == 0
    else:
        order = [lax.rem(z + i, n_sec) for i in range(1, n_sec + 1)]

    def units_of(j):
        if j == sectors - 1:
            parts = 4
        elif j == 0:
            parts = 2
        else:
            return [None]
        each = n_sec // parts
        return [order[i * each:(i + 1) * each] for i in range(parts)]

    def psi_copy(j):
        return pltpu.make_async_copy(psi_hbm.at[j], psi.at[j], psi_sem.at[j])

    def right_copy(j):
        return pltpu.make_async_copy(right_hbm.at[j], right.at[j], right_sem.at[j])

    def own_copy(j):
        return pltpu.make_async_copy(left_hbm.at[o, j], left.at[j, o], own_sem.at[j])

    def rows_of(block):
        if block is None:
            return pl.ds(0, width)
        return pl.ds(pl.multiple_of(block * rows, rows), rows)

    def left_copy(j, block, peer, slot):
        which = 0 if block is None else block
        return pltpu.make_async_remote_copy(
            src_ref=left_hbm.at[peer, j, rows_of(block)],
            dst_ref=left.at[j, slot, rows_of(block)],
            send_sem=lsend_sem.at[j, which, peer], recv_sem=lrecv_sem.at[j, which, slot],
            device_id=(peer, z), device_id_type=MESH,
        )

    def part_copy(j, peer, slot):
        return pltpu.make_async_remote_copy(
            src_ref=zsend.at[j, rows_of(peer)], dst_ref=zrecv.at[j, slot],
            send_sem=zsend_sem.at[j, peer], recv_sem=zrecv_sem.at[j, slot],
            device_id=(o, peer), device_id_type=MESH,
        )

    def relay_copy(j):
        return pltpu.make_async_remote_copy(
            src_ref=zsend.at[j, rows_of(far)], dst_ref=relayed.at[j],
            send_sem=zsend_sem.at[j, far], recv_sem=relay_sem.at[j],
            device_id=(o, beside), device_id_type=MESH,
        )

    def op_peers(body):
        def step(i, _):
            body(lax.rem(o + i, n_op))
            return 0
        lax.fori_loop(1, n_op, step, 0)

    def sec_peers(body):
        def step(i, _):
            body(lax.rem(z + i, n_sec))
            return 0
        lax.fori_loop(1, n_sec, step, 0)

    def left_blocks(j):
        return [block for unit in units_of(j) for block in (unit or [None])]

    barrier = pltpu.get_barrier_semaphore()
    op_peers(lambda peer: pl.semaphore_signal(
        barrier, inc=1, device_id=(peer, z), device_id_type=MESH))
    sec_peers(lambda peer: pl.semaphore_signal(
        barrier, inc=1, device_id=(o, peer), device_id_type=MESH))
    for j in range(sectors):
        psi_copy(j).start()
        right_copy(j).start()
        own_copy(j).start()
    pl.semaphore_wait(barrier, n_op + n_sec - 2)

    for j in range(sectors):
        for block in left_blocks(j):
            op_peers(lambda peer: left_copy(j, block, peer, o).start())

    def mask_of(j, first, height):
        size = dims_ref[o * sectors + j]
        down = lax.broadcasted_iota(jnp.int32, (height, width), 0) + first
        across = lax.broadcasted_iota(jnp.int32, (height, width), 1)
        return jnp.where((down < size) & (across < size), 1.0, 0.0).astype(jnp.float32)

    def mix(j):
        psi_copy(j).wait()
        right_copy(j).wait()
        inside = mask_of(j, 0, width).astype(jnp.bfloat16)
        for p in range(p_size):
            psi[j, p] = psi[j, p] * inside

        def one_term(a, _):
            block = right[j, a]
            term = a * n_sec + z
            weights = [[site_ref[q, p, term] for p in range(p_size)] for q in range(p_size)]
            for c in range(width // chunk):
                here = pl.ds(c * chunk, chunk)
                waves = psi[j, :, here, :].reshape(p_size * chunk, width)
                got = lax.dot_general(
                    waves, block, (((1,), (1,)), ((), ())), preferred_element_type=jnp.float32
                )
                for q in range(p_size):
                    value = weights[q][0] * got[:chunk]
                    for p in range(1, p_size):
                        value = value + weights[q][p] * got[p * chunk:(p + 1) * chunk]
                    mixed[j, a, here, pl.ds(q * width, width)] = value.astype(jnp.bfloat16)
            return 0

        lax.fori_loop(0, n_op, one_term, 0)

    def send_part(j, block):
        if not relays:
            part_copy(j, block, z).start()
        elif block is far:
            @pl.when(outer)
            def _():
                relay_copy(j).start()
        else:
            part_copy(j, block, z).start()

    def relay(j):
        if not relays:
            return

        @pl.when(jnp.logical_not(outer))
        def _():
            relay_copy(j).wait_recv()
            value = total[j, rows_of(far), :] + relayed[j].astype(jnp.float32)
            zsend[j, rows_of(far), :] = value.astype(jnp.bfloat16)
            part_copy(j, far, z).start()

    def contract(j, unit):
        blocks = unit or [None]
        for block in blocks:
            op_peers(lambda peer: left_copy(j, block, peer, peer).wait_recv())

        def left_rows(a):
            parts = [left[j, a, rows_of(block), :] for block in blocks]
            return parts[0] if len(parts) == 1 else jnp.concatenate(parts, axis=0)

        def one_state(q, _):
            cols = pl.ds(pl.multiple_of(q * width, width), width)
            value = jnp.dot(
                left_rows(0), mixed[j, 0, :, cols], preferred_element_type=jnp.float32
            )
            for a in range(1, n_op):
                value = value + jnp.dot(
                    left_rows(a), mixed[j, a, :, cols], preferred_element_type=jnp.float32
                )
            height = value.shape[0] // len(blocks)
            for i, block in enumerate(blocks):
                part = value[i * height:(i + 1) * height]
                total[j, rows_of(block), cols] = part
                zsend[j, rows_of(block), cols] = part.astype(jnp.bfloat16)
            return 0

        lax.fori_loop(0, p_size, one_state, 0)
        for block in (unit or order):
            if block is not order[-1]:
                send_part(j, block)

    def finish(j):
        own = rows_of(z)
        inside = mask_of(j, z * rows, rows)
        if relays:
            part_copy(j, 2 - half, 2 - half).wait_recv()
            part_copy(j, beside, beside).wait_recv()

            @pl.when(jnp.logical_not(outer))
            def _():
                part_copy(j, far, far).wait_recv()
                total[j, own, :] = total[j, own, :] + zrecv[j, far].astype(jnp.float32)

            peers = [2 - half, beside]
        else:
            sec_peers(lambda peer: part_copy(j, peer, peer).wait_recv())
            peers = order[:-1]
        for q in range(p_size):
            cols = pl.ds(q * width, width)
            value = total[j, own, cols]
            for peer in peers:
                value = value + zrecv[j, peer, :, cols].astype(jnp.float32)
            out_ref[j, :, cols] = (value * inside).astype(jnp.bfloat16)

    mix(0)
    last = sectors - 1
    for j in range(sectors):
        if j < last:
            mix(j + 1)
        if j == last:
            for i in range(last - 1):
                finish(i)
        own_copy(j).wait()
        for i, unit in enumerate(units_of(j)):
            contract(j, unit)
            if i == 0 and j > 0:
                relay(j - 1)
            if i == 1 and j == last:
                relay(j)
    for j in range(max(last - 1, 0), sectors):
        finish(j)

    for j in range(sectors):
        for block in left_blocks(j):
            op_peers(lambda peer: left_copy(j, block, peer, o).wait_send())
        sec_peers(lambda peer: part_copy(j, peer, z).wait_send())


def shards(wave, sector_dims, left_ops, right_ops, site_ops):
    n_op = lax.axis_size("op")
    n_sec = lax.axis_size("sec")
    sectors, width, p_size = wave.shape[0], wave.shape[1], wave.shape[2]
    rows = width // n_sec
    waves = jnp.transpose(wave, (0, 2, 1, 3))
    left = left_ops.reshape(n_op, sectors, width, width)
    right = right_ops.reshape(sectors, n_op, width, width)
    sites = jnp.transpose(site_ops, (1, 2, 0))
    wide = p_size * width
    flops = 4 * sectors * n_op * width * width * wide
    sigma = pl.pallas_call(
        functools.partial(kernel, n_op, n_sec),
        out_shape=jax.ShapeDtypeStruct((sectors, rows, wide), jnp.bfloat16),
        in_specs=[
            pl.BlockSpec(memory_space=pltpu.SMEM),
            pl.BlockSpec(memory_space=pltpu.SMEM),
            pl.BlockSpec(memory_space=pl.ANY),
            pl.BlockSpec(memory_space=pl.ANY),
            pl.BlockSpec(memory_space=pl.ANY),
        ],
        out_specs=pl.BlockSpec(memory_space=pltpu.VMEM),
        scratch_shapes=[
            pltpu.VMEM((sectors, p_size, width, width), jnp.bfloat16),
            pltpu.VMEM((sectors, n_op, width, width), jnp.bfloat16),
            pltpu.VMEM((sectors, n_op, width, width), jnp.bfloat16),
            pltpu.VMEM((sectors, n_op, width, wide), jnp.bfloat16),
            pltpu.VMEM((sectors, width, wide), jnp.float32),
            pltpu.VMEM((sectors, width, wide), jnp.bfloat16),
            pltpu.VMEM((sectors, n_sec, rows, wide), jnp.bfloat16),
            pltpu.VMEM((sectors, rows, wide), jnp.bfloat16),
            pltpu.SemaphoreType.DMA((sectors,)),
            pltpu.SemaphoreType.DMA((sectors,)),
            pltpu.SemaphoreType.DMA((sectors,)),
            pltpu.SemaphoreType.DMA((sectors, n_sec, n_op)),
            pltpu.SemaphoreType.DMA((sectors, n_sec, n_op)),
            pltpu.SemaphoreType.DMA((sectors, n_sec)),
            pltpu.SemaphoreType.DMA((sectors, n_sec)),
            pltpu.SemaphoreType.DMA((sectors,)),
        ],
        compiler_params=pltpu.CompilerParams(
            collective_id=0, has_side_effects=True, vmem_limit_bytes=48 * MIB
        ),
        cost_estimate=pl.CostEstimate(flops=flops, bytes_accessed=12 * MIB, transcendentals=0),
    )(sites, sector_dims, waves, left, right)
    return sigma.reshape(sectors, rows, p_size, width)


def solution(mesh):
    placed = (
        P("op", None, None, None),
        P(),
        P(None, ("op", "sec"), None, None),
        P("op", None, "sec", None, None),
        P(),
    )
    return jax.shard_map(
        shards, mesh=mesh, in_specs=placed, out_specs=P("op", "sec", None, None), check_vma=False
    )
```

```python
import functools

import jax
import jax.numpy as jnp
from jax import lax
from jax.experimental import pallas as pl
from jax.experimental.pallas import tpu as pltpu
from jax.sharding import PartitionSpec as P

MESH = pl.DeviceIdType.MESH
MIB = 1024 * 1024
AHEAD = 3
CHUNK = 64


def kernel(
    n_op, n_sec, site_ref, dims_ref, psi_hbm, left_hbm, right_hbm, out_ref,
    psi, right, left, mixed, total, zsend, zrecv, relayed,
    psi_sem, right_sem, own_sem, lsend_sem, lrecv_sem, zsend_sem, zrecv_sem, relay_sem,
):
    o = lax.axis_index("op")
    z = lax.axis_index("sec")
    sectors, p_size, width = psi.shape[0], psi.shape[1], psi.shape[2]
    rows = width // n_sec
    tall = width // 2
    per_half = n_sec // 2
    relays = n_sec == 4

    own_half = z // per_half
    halves = [1 - own_half, own_half]
    beside = z + 1 - 2 * lax.rem(z, 2)
    far = 3 * halves[0]
    near = 1 + halves[0]
    outer = lax.rem(z, 3) == 0

    def psi_copy(j):
        return pltpu.make_async_copy(psi_hbm.at[j], psi.at[j], psi_sem.at[j])

    def right_copy(j):
        return pltpu.make_async_copy(right_hbm.at[j], right.at[j], right_sem.at[j])

    def own_copy(j):
        return pltpu.make_async_copy(left_hbm.at[o, j], left.at[j, o], own_sem.at[j])

    def rows_of(block):
        return pl.ds(pl.multiple_of(block * rows, rows), rows)

    def half_of(half):
        return pl.ds(pl.multiple_of(half * tall, tall), tall)

    def left_copy(j, half, peer, slot):
        return pltpu.make_async_remote_copy(
            src_ref=left_hbm.at[peer, j, half_of(half)],
            dst_ref=left.at[j, slot, half_of(half)],
            send_sem=lsend_sem.at[j, half, peer], recv_sem=lrecv_sem.at[j, half, slot],
            device_id=(peer, z), device_id_type=MESH,
        )

    def part_copy(j, peer, slot):
        return pltpu.make_async_remote_copy(
            src_ref=zsend.at[j, rows_of(peer)], dst_ref=zrecv.at[j, slot],
            send_sem=zsend_sem.at[j, peer], recv_sem=zrecv_sem.at[j, slot],
            device_id=(o, peer), device_id_type=MESH,
        )

    def relay_copy(j):
        return pltpu.make_async_remote_copy(
            src_ref=zsend.at[j, rows_of(far)], dst_ref=relayed.at[j],
            send_sem=zsend_sem.at[j, far], recv_sem=relay_sem.at[j],
            device_id=(o, beside), device_id_type=MESH,
        )

    def op_peers(body):
        def step(i, _):
            body(lax.rem(o + i, n_op))
            return 0
        lax.fori_loop(1, n_op, step, 0)

    def sec_peers(body):
        def step(i, _):
            body(lax.rem(z + i, n_sec))
            return 0
        lax.fori_loop(1, n_sec, step, 0)

    steps = [(j, half) for j in range(sectors) for half in halves]

    def send_left(index):
        if index < len(steps):
            j, half = steps[index]
            op_peers(lambda peer: left_copy(j, half, peer, o).start())

    barrier = pltpu.get_barrier_semaphore()
    op_peers(lambda peer: pl.semaphore_signal(
        barrier, inc=1, device_id=(peer, z), device_id_type=MESH))
    sec_peers(lambda peer: pl.semaphore_signal(
        barrier, inc=1, device_id=(o, peer), device_id_type=MESH))
    for j in range(sectors):
        psi_copy(j).start()
        right_copy(j).start()
        own_copy(j).start()
    pl.semaphore_wait(barrier, n_op + n_sec - 2)

    for index in range(AHEAD):
        send_left(index)

    def mask_of(j, first, height):
        size = dims_ref[o * sectors + j]
        down = lax.broadcasted_iota(jnp.int32, (height, width), 0) + first
        across = lax.broadcasted_iota(jnp.int32, (height, width), 1)
        return jnp.where((down < size) & (across < size), 1.0, 0.0).astype(jnp.float32)

    def mix(j):
        psi_copy(j).wait()
        right_copy(j).wait()
        inside = mask_of(j, 0, width).astype(jnp.bfloat16)
        for p in range(p_size):
            psi[j, p] = psi[j, p] * inside

        def one_term(a, _):
            block = right[j, a]
            term = a * n_sec + z
            weights = [[site_ref[q, p, term] for p in range(p_size)] for q in range(p_size)]
            got = lax.dot_general(
                psi[j].reshape(p_size * width, width), block, (((1,), (1,)), ((), ())),
                preferred_element_type=jnp.float32,
            )
            for c in range(width // CHUNK):
                parts = [
                    got[p * width + c * CHUNK:p * width + (c + 1) * CHUNK] for p in range(p_size)
                ]
                for q in range(p_size):
                    value = weights[q][0] * parts[0]
                    for p in range(1, p_size):
                        value = value + weights[q][p] * parts[p]
                    mixed[j, a, pl.ds(c * CHUNK, CHUNK), pl.ds(q * width, width)] = value.astype(
                        jnp.bfloat16
                    )
            return 0

        lax.fori_loop(0, n_op, one_term, 0)

    def send_half(j, first):
        if relays:
            if first:
                @pl.when(outer)
                def _():
                    relay_copy(j).start()

                part_copy(j, near, z).start()
            else:
                part_copy(j, beside, z).start()
        elif first:
            for i in range(per_half):
                part_copy(j, halves[0] * per_half + i, z).start()
        else:
            for i in range(1, per_half):
                part_copy(j, own_half * per_half + lax.rem(z + i, per_half), z).start()

    def relay(j):
        if not relays:
            return

        @pl.when(jnp.logical_not(outer))
        def _():
            relay_copy(j).wait_recv()
            value = total[j, rows_of(far), :] + relayed[j].astype(jnp.float32)
            zsend[j, rows_of(far), :] = value.astype(jnp.bfloat16)
            part_copy(j, far, z).start()

    def contract(index):
        j, half = steps[index]
        op_peers(lambda peer: left_copy(j, half, peer, peer).wait_recv())
        op_peers(lambda peer: left_copy(j, half, peer, o).wait_send())
        send_left(index + AHEAD)
        here = half_of(half)

        def one_state(q, _):
            cols = pl.ds(pl.multiple_of(q * width, width), width)
            value = jnp.dot(
                jnp.concatenate([left[j, a, here, :] for a in range(n_op)], axis=1),
                mixed[j, :, :, cols].reshape(n_op * width, width),
                preferred_element_type=jnp.float32,
            )
            total[j, here, cols] = value
            zsend[j, here, cols] = value.astype(jnp.bfloat16)
            return 0

        lax.fori_loop(0, p_size, one_state, 0)
        send_half(j, index % 2 == 0)

    def finish(j):
        own = rows_of(z)
        inside = mask_of(j, z * rows, rows)
        if relays:
            part_copy(j, near, near).wait_recv()
            part_copy(j, beside, beside).wait_recv()

            @pl.when(jnp.logical_not(outer))
            def _():
                part_copy(j, far, far).wait_recv()
                total[j, own, :] = total[j, own, :] + zrecv[j, far].astype(jnp.float32)

            peers = [near, beside]
        else:
            sec_peers(lambda peer: part_copy(j, peer, peer).wait_recv())
            peers = [lax.rem(z + i, n_sec) for i in range(1, n_sec)]
        for q in range(p_size):
            cols = pl.ds(q * width, width)
            value = total[j, own, cols]
            for peer in peers:
                value = value + zrecv[j, peer, :, cols].astype(jnp.float32)
            out_ref[j, :, cols] = (value * inside).astype(jnp.bfloat16)

    mix(0)
    last = sectors - 1
    for j in range(sectors):
        if j < last:
            mix(j + 1)
        if j == last:
            for i in range(last - 1):
                finish(i)
        own_copy(j).wait()
        contract(2 * j)
        if j > 0:
            relay(j - 1)
        if j == last:
            relay(j)
        contract(2 * j + 1)
    for j in range(max(last - 1, 0), sectors):
        finish(j)

    for j in range(sectors):
        sec_peers(lambda peer: part_copy(j, peer, z).wait_send())


def shards(wave, sector_dims, left_ops, right_ops, site_ops):
    n_op = lax.axis_size("op")
    n_sec = lax.axis_size("sec")
    sectors, width, p_size = wave.shape[0], wave.shape[1], wave.shape[2]
    rows = width // n_sec
    waves = jnp.transpose(wave, (0, 2, 1, 3))
    left = left_ops.reshape(n_op, sectors, width, width)
    right = right_ops.reshape(sectors, n_op, width, width)
    sites = jnp.transpose(site_ops, (1, 2, 0))
    wide = p_size * width
    flops = 4 * sectors * n_op * width * width * wide
    sigma = pl.pallas_call(
        functools.partial(kernel, n_op, n_sec),
        out_shape=jax.ShapeDtypeStruct((sectors, rows, wide), jnp.bfloat16),
        in_specs=[
            pl.BlockSpec(memory_space=pltpu.SMEM),
            pl.BlockSpec(memory_space=pltpu.SMEM),
            pl.BlockSpec(memory_space=pl.ANY),
            pl.BlockSpec(memory_space=pl.ANY),
            pl.BlockSpec(memory_space=pl.ANY),
        ],
        out_specs=pl.BlockSpec(memory_space=pltpu.VMEM),
        scratch_shapes=[
            pltpu.VMEM((sectors, p_size, width, width), jnp.bfloat16),
            pltpu.VMEM((sectors, n_op, width, width), jnp.bfloat16),
            pltpu.VMEM((sectors, n_op, width, width), jnp.bfloat16),
            pltpu.VMEM((sectors, n_op, width, wide), jnp.bfloat16),
            pltpu.VMEM((sectors, width, wide), jnp.float32),
            pltpu.VMEM((sectors, width, wide), jnp.bfloat16),
            pltpu.VMEM((sectors, n_sec, rows, wide), jnp.bfloat16),
            pltpu.VMEM((sectors, rows, wide), jnp.bfloat16),
            pltpu.SemaphoreType.DMA((sectors,)),
            pltpu.SemaphoreType.DMA((sectors,)),
            pltpu.SemaphoreType.DMA((sectors,)),
            pltpu.SemaphoreType.DMA((sectors, 2, n_op)),
            pltpu.SemaphoreType.DMA((sectors, 2, n_op)),
            pltpu.SemaphoreType.DMA((sectors, n_sec)),
            pltpu.SemaphoreType.DMA((sectors, n_sec)),
            pltpu.SemaphoreType.DMA((sectors,)),
        ],
        compiler_params=pltpu.CompilerParams(
            collective_id=0, has_side_effects=True, vmem_limit_bytes=48 * MIB
        ),
        cost_estimate=pl.CostEstimate(flops=flops, bytes_accessed=12 * MIB, transcendentals=0),
    )(sites, sector_dims, waves, left, right)
    return sigma.reshape(sectors, rows, p_size, width)


def solution(mesh):
    placed = (
        P("op", None, None, None),
        P(),
        P(None, ("op", "sec"), None, None),
        P("op", None, "sec", None, None),
        P(),
    )
    return jax.shard_map(
        shards, mesh=mesh, in_specs=placed, out_specs=P("op", "sec", None, None), check_vma=False
    )
```

```python
import functools

import jax
import jax.numpy as jnp
from jax import lax
from jax.experimental import pallas as pl
from jax.experimental.pallas import tpu as pltpu
from jax.sharding import PartitionSpec as P

MESH = pl.DeviceIdType.MESH
MIB = 1024 * 1024
AHEAD = 4
CHUNK = 64


def kernel(
    n_op, n_sec, site_ref, dims_ref, wave_hbm, left_hbm, right_hbm, out_ref,
    wave, psi, right, left, mixed, total, zsend, zrecv, relayed,
    wave_sem, right_sem, own_sem, lsend_sem, lrecv_sem, zsend_sem, zrecv_sem, relay_sem,
):
    o = lax.axis_index("op")
    z = lax.axis_index("sec")
    sectors, p_size, width = psi.shape[0], psi.shape[1], psi.shape[2]
    rows = width // n_sec
    tall = width // 2
    per_half = n_sec // 2
    relays = n_sec == 4

    own_half = z // per_half
    halves = [1 - own_half, own_half]
    beside = z + 1 - 2 * lax.rem(z, 2)
    far = 3 * halves[0]
    near = 1 + halves[0]
    outer = lax.rem(z, 3) == 0

    def wave_copy(j):
        return pltpu.make_async_copy(wave_hbm.at[j], wave.at[j], wave_sem.at[j])

    def right_copy(j):
        return pltpu.make_async_copy(right_hbm.at[j], right.at[j], right_sem.at[j])

    def own_copy(j):
        return pltpu.make_async_copy(left_hbm.at[o, j], left.at[j, o], own_sem.at[j])

    def rows_of(block):
        return pl.ds(pl.multiple_of(block * rows, rows), rows)

    def left_copy(step, peer, slot):
        j, piece, first, height, _ = step
        here = pl.ds(pl.multiple_of(first, height), height)
        return pltpu.make_async_remote_copy(
            src_ref=left_hbm.at[peer, j, here],
            dst_ref=left.at[j, slot, here],
            send_sem=lsend_sem.at[j, piece, peer], recv_sem=lrecv_sem.at[j, piece, slot],
            device_id=(peer, z), device_id_type=MESH,
        )

    def part_copy(j, peer, slot):
        return pltpu.make_async_remote_copy(
            src_ref=zsend.at[j, rows_of(peer)], dst_ref=zrecv.at[j, slot],
            send_sem=zsend_sem.at[j, peer], recv_sem=zrecv_sem.at[j, slot],
            device_id=(o, peer), device_id_type=MESH,
        )

    def relay_copy(j):
        return pltpu.make_async_remote_copy(
            src_ref=zsend.at[j, rows_of(far)], dst_ref=relayed.at[j],
            send_sem=zsend_sem.at[j, far], recv_sem=relay_sem.at[j],
            device_id=(o, beside), device_id_type=MESH,
        )

    def op_peers(body):
        def step(i, _):
            body(lax.rem(o + i, n_op))
            return 0
        lax.fori_loop(1, n_op, step, 0)

    def sec_peers(body):
        def step(i, _):
            body(lax.rem(z + i, n_sec))
            return 0
        lax.fori_loop(1, n_sec, step, 0)

    steps = []
    for j in range(sectors):
        steps.append((j, 0, halves[0] * tall, tall, "other"))
        if relays and j == sectors - 1:
            steps.append((j, 1, beside * rows, rows, "beside"))
            steps.append((j, 2, z * rows, rows, "none"))
        else:
            steps.append((j, 1, halves[1] * tall, tall, "beside"))

    def send_left(index):
        if index < len(steps):
            op_peers(lambda peer: left_copy(steps[index], peer, o).start())

    barrier = pltpu.get_barrier_semaphore()
    op_peers(lambda peer: pl.semaphore_signal(
        barrier, inc=1, device_id=(peer, z), device_id_type=MESH))
    sec_peers(lambda peer: pl.semaphore_signal(
        barrier, inc=1, device_id=(o, peer), device_id_type=MESH))
    for j in range(sectors):
        wave_copy(j).start()
        right_copy(j).start()
        own_copy(j).start()
    pl.semaphore_wait(barrier, n_op + n_sec - 2)

    for index in range(AHEAD):
        send_left(index)

    def mask_of(j, first, height):
        size = dims_ref[o * sectors + j]
        down = lax.broadcasted_iota(jnp.int32, (height, width), 0) + first
        across = lax.broadcasted_iota(jnp.int32, (height, width), 1)
        return jnp.where((down < size) & (across < size), 1.0, 0.0).astype(jnp.float32)

    def mix(j):
        wave_copy(j).wait()
        right_copy(j).wait()

        def lay_out(c, _):
            here = pl.ds(pl.multiple_of(c * CHUNK, CHUNK), CHUNK)
            inside = mask_of(j, c * CHUNK, CHUNK).astype(jnp.bfloat16)
            psi[j, :, here, :] = jnp.swapaxes(wave[j, here], 0, 1) * inside[None]
            return 0

        lax.fori_loop(0, width // CHUNK, lay_out, 0)

        def one_term(a, _):
            block = right[j, a]
            term = a * n_sec + z
            weights = [[site_ref[q, p, term] for p in range(p_size)] for q in range(p_size)]
            got = lax.dot_general(
                psi[j].reshape(p_size * width, width), block, (((1,), (1,)), ((), ())),
                preferred_element_type=jnp.float32,
            )
            for c in range(width // CHUNK):
                parts = [
                    got[p * width + c * CHUNK:p * width + (c + 1) * CHUNK] for p in range(p_size)
                ]
                for q in range(p_size):
                    value = weights[q][0] * parts[0]
                    for p in range(1, p_size):
                        value = value + weights[q][p] * parts[p]
                    mixed[j, a, pl.ds(c * CHUNK, CHUNK), pl.ds(q * width, width)] = value.astype(
                        jnp.bfloat16
                    )
            return 0

        lax.fori_loop(0, n_op, one_term, 0)

    def send_parts(j, which):
        if which == "none":
            return
        if relays:
            if which == "other":
                @pl.when(outer)
                def _():
                    relay_copy(j).start()

                part_copy(j, near, z).start()
            else:
                part_copy(j, beside, z).start()
        elif which == "other":
            for i in range(per_half):
                part_copy(j, halves[0] * per_half + i, z).start()
        else:
            for i in range(1, per_half):
                part_copy(j, own_half * per_half + lax.rem(z + i, per_half), z).start()

    def relay(j):
        if not relays:
            return

        @pl.when(jnp.logical_not(outer))
        def _():
            relay_copy(j).wait_recv()
            value = total[j, rows_of(far), :] + relayed[j].astype(jnp.float32)
            zsend[j, rows_of(far), :] = value.astype(jnp.bfloat16)
            part_copy(j, far, z).start()

    def contract(index):
        step = steps[index]
        j, _, first, height, which = step
        op_peers(lambda peer: left_copy(step, peer, peer).wait_recv())
        op_peers(lambda peer: left_copy(step, peer, o).wait_send())
        send_left(index + AHEAD)
        here = pl.ds(pl.multiple_of(first, height), height)

        def one_state(q, _):
            cols = pl.ds(pl.multiple_of(q * width, width), width)
            value = jnp.dot(
                jnp.concatenate([left[j, a, here, :] for a in range(n_op)], axis=1),
                mixed[j, :, :, cols].reshape(n_op * width, width),
                preferred_element_type=jnp.float32,
            )
            total[j, here, cols] = value
            zsend[j, here, cols] = value.astype(jnp.bfloat16)
            return 0

        lax.fori_loop(0, p_size, one_state, 0)
        send_parts(j, which)

    def finish(j):
        own = rows_of(z)
        inside = mask_of(j, z * rows, rows)
        if relays:
            part_copy(j, near, near).wait_recv()
            part_copy(j, beside, beside).wait_recv()

            @pl.when(jnp.logical_not(outer))
            def _():
                part_copy(j, far, far).wait_recv()
                total[j, own, :] = total[j, own, :] + zrecv[j, far].astype(jnp.float32)

            peers = [near, beside]
        else:
            sec_peers(lambda peer: part_copy(j, peer, peer).wait_recv())
            peers = [lax.rem(z + i, n_sec) for i in range(1, n_sec)]
        states = []
        for q in range(p_size):
            cols = pl.ds(q * width, width)
            value = total[j, own, cols]
            for peer in peers:
                value = value + zrecv[j, peer, :, cols].astype(jnp.float32)
            states.append((value * inside).astype(jnp.bfloat16))
        out_ref[j] = jnp.swapaxes(jnp.stack(states), 0, 1)

    mix(0)
    last = sectors - 1
    for j in range(sectors):
        if j < last:
            mix(j + 1)
        if j == last:
            for i in range(last - 1):
                finish(i)
        own_copy(j).wait()
        contract(2 * j)
        if j > 0:
            relay(j - 1)
        if j == last:
            relay(j)
        contract(2 * j + 1)
    if last > 0:
        finish(last - 1)
    if relays:
        contract(2 * sectors)
    finish(last)

    for j in range(sectors):
        sec_peers(lambda peer: part_copy(j, peer, z).wait_send())


def shards(wave, sector_dims, left_ops, right_ops, site_ops):
    n_op = lax.axis_size("op")
    n_sec = lax.axis_size("sec")
    sectors, width, p_size = wave.shape[0], wave.shape[1], wave.shape[2]
    rows = width // n_sec
    left = left_ops.reshape(n_op, sectors, width, width)
    right = right_ops.reshape(sectors, n_op, width, width)
    sites = jnp.transpose(site_ops, (1, 2, 0))
    wide = p_size * width
    flops = 4 * sectors * n_op * width * width * wide
    return pl.pallas_call(
        functools.partial(kernel, n_op, n_sec),
        out_shape=jax.ShapeDtypeStruct((sectors, rows, p_size, width), jnp.bfloat16),
        in_specs=[
            pl.BlockSpec(memory_space=pltpu.SMEM),
            pl.BlockSpec(memory_space=pltpu.SMEM),
            pl.BlockSpec(memory_space=pl.ANY),
            pl.BlockSpec(memory_space=pl.ANY),
            pl.BlockSpec(memory_space=pl.ANY),
        ],
        out_specs=pl.BlockSpec(memory_space=pltpu.VMEM),
        scratch_shapes=[
            pltpu.VMEM((sectors, width, p_size, width), jnp.bfloat16),
            pltpu.VMEM((sectors, p_size, width, width), jnp.bfloat16),
            pltpu.VMEM((sectors, n_op, width, width), jnp.bfloat16),
            pltpu.VMEM((sectors, n_op, width, width), jnp.bfloat16),
            pltpu.VMEM((sectors, n_op, width, wide), jnp.bfloat16),
            pltpu.VMEM((sectors, width, wide), jnp.float32),
            pltpu.VMEM((sectors, width, wide), jnp.bfloat16),
            pltpu.VMEM((sectors, n_sec, rows, wide), jnp.bfloat16),
            pltpu.VMEM((sectors, rows, wide), jnp.bfloat16),
            pltpu.SemaphoreType.DMA((sectors,)),
            pltpu.SemaphoreType.DMA((sectors,)),
            pltpu.SemaphoreType.DMA((sectors,)),
            pltpu.SemaphoreType.DMA((sectors, 3, n_op)),
            pltpu.SemaphoreType.DMA((sectors, 3, n_op)),
            pltpu.SemaphoreType.DMA((sectors, n_sec)),
            pltpu.SemaphoreType.DMA((sectors, n_sec)),
            pltpu.SemaphoreType.DMA((sectors,)),
        ],
        compiler_params=pltpu.CompilerParams(
            collective_id=0, has_side_effects=True, vmem_limit_bytes=56 * MIB
        ),
        cost_estimate=pl.CostEstimate(flops=flops, bytes_accessed=12 * MIB, transcendentals=0),
    )(sites, sector_dims, wave, left, right)


def solution(mesh):
    placed = (
        P("op", None, None, None),
        P(),
        P(None, ("op", "sec"), None, None),
        P("op", None, "sec", None, None),
        P(),
    )
    return jax.shard_map(
        shards, mesh=mesh, in_specs=placed, out_specs=P("op", "sec", None, None), check_vma=False
    )
```

```python
import functools

import jax
import jax.numpy as jnp
from jax import lax
from jax.experimental import pallas as pl
from jax.experimental.pallas import tpu as pltpu
from jax.sharding import PartitionSpec as P

MESH = pl.DeviceIdType.MESH
MIB = 1024 * 1024
AHEAD = 4
CHUNK = 64


def kernel(
    n_op, n_sec, site_ref, dims_ref, wave_hbm, left_hbm, right_hbm, out_ref,
    wave, psi, right, left, mixed, total, zsend, zrecv, relayed,
    wave_sem, right_sem, own_sem, lsend_sem, lrecv_sem, zsend_sem, zrecv_sem, relay_sem,
):
    o = lax.axis_index("op")
    z = lax.axis_index("sec")
    sectors, width, p_size = wave.shape[0], wave.shape[1], wave.shape[2]
    chunks = width // CHUNK
    rows = width // n_sec
    tall = width // 2
    per_half = n_sec // 2
    relays = n_sec == 4

    own_half = z // per_half
    halves = [1 - own_half, own_half]
    beside = z + 1 - 2 * lax.rem(z, 2)
    far = 3 * halves[0]
    near = 1 + halves[0]
    outer = lax.rem(z, 3) == 0

    def wave_copy(j):
        return pltpu.make_async_copy(wave_hbm.at[j], wave.at[j], wave_sem.at[j])

    def right_copy(j):
        return pltpu.make_async_copy(right_hbm.at[j], right.at[j], right_sem.at[j])

    def own_copy(j):
        return pltpu.make_async_copy(left_hbm.at[o, j], left.at[j, o], own_sem.at[j])

    def rows_of(block):
        return pl.ds(pl.multiple_of(block * rows, rows), rows)

    def left_copy(step, peer, slot):
        j, piece, first, height = step
        here = pl.ds(pl.multiple_of(first, height), height)
        return pltpu.make_async_remote_copy(
            src_ref=left_hbm.at[peer, j, here],
            dst_ref=left.at[j, slot, here],
            send_sem=lsend_sem.at[j, piece, peer], recv_sem=lrecv_sem.at[j, piece, slot],
            device_id=(peer, z), device_id_type=MESH,
        )

    def part_copy(j, peer, slot):
        return pltpu.make_async_remote_copy(
            src_ref=zsend.at[j, rows_of(peer)], dst_ref=zrecv.at[j, slot],
            send_sem=zsend_sem.at[j, peer], recv_sem=zrecv_sem.at[j, slot],
            device_id=(o, peer), device_id_type=MESH,
        )

    def relay_copy(j):
        return pltpu.make_async_remote_copy(
            src_ref=zsend.at[j, rows_of(far)], dst_ref=relayed.at[j],
            send_sem=zsend_sem.at[j, far], recv_sem=relay_sem.at[j],
            device_id=(o, beside), device_id_type=MESH,
        )

    def op_peers(body):
        def step(i, _):
            body(lax.rem(o + i, n_op))
            return 0
        lax.fori_loop(1, n_op, step, 0)

    def sec_peers(body):
        def step(i, _):
            body(lax.rem(z + i, n_sec))
            return 0
        lax.fori_loop(1, n_sec, step, 0)

    steps = []
    for j in range(sectors):
        steps.append((j, 0, halves[0] * tall, tall))
        if relays and j == sectors - 1:
            steps.append((j, 1, beside * rows, rows))
            steps.append((j, 2, z * rows, rows))
        else:
            steps.append((j, 1, halves[1] * tall, tall))

    def send_left(index):
        if index < len(steps):
            op_peers(lambda peer: left_copy(steps[index], peer, o).start())

    barrier = pltpu.get_barrier_semaphore()
    op_peers(lambda peer: pl.semaphore_signal(
        barrier, inc=1, device_id=(peer, z), device_id_type=MESH))
    sec_peers(lambda peer: pl.semaphore_signal(
        barrier, inc=1, device_id=(o, peer), device_id_type=MESH))
    for j in range(sectors):
        wave_copy(j).start()
        right_copy(j).start()
        own_copy(j).start()
    pl.semaphore_wait(barrier, n_op + n_sec - 2)

    for index in range(AHEAD):
        send_left(index)

    def mask_of(j, first, height):
        size = dims_ref[o * sectors + j]
        down = lax.broadcasted_iota(jnp.int32, (height, width), 0) + first
        across = lax.broadcasted_iota(jnp.int32, (height, width), 1)
        return jnp.where((down < size) & (across < size), 1.0, 0.0).astype(jnp.float32)

    def mix(j):
        wave_copy(j).wait()
        right_copy(j).wait()

        def lay_out(c, _):
            here = pl.ds(pl.multiple_of(c * CHUNK, CHUNK), CHUNK)
            inside = mask_of(j, c * CHUNK, CHUNK).astype(jnp.bfloat16)
            psi[j, c] = jnp.swapaxes(wave[j, here], 0, 1) * inside[None]
            return 0

        lax.fori_loop(0, chunks, lay_out, 0)

        def one_term(a, _):
            block = right[j, a]
            term = a * n_sec + z
            weights = [[site_ref[q, p, term] for p in range(p_size)] for q in range(p_size)]
            got = lax.dot_general(
                psi[j].reshape(p_size * width, width), block, (((1,), (1,)), ((), ())),
                preferred_element_type=jnp.float32,
            )
            for c in range(chunks):
                parts = [
                    got[(c * p_size + p) * CHUNK:(c * p_size + p + 1) * CHUNK]
                    for p in range(p_size)
                ]
                for q in range(p_size):
                    value = weights[q][0] * parts[0]
                    for p in range(1, p_size):
                        value = value + weights[q][p] * parts[p]
                    mixed[j, a, pl.ds(c * CHUNK, CHUNK), pl.ds(q * width, width)] = value.astype(
                        jnp.bfloat16
                    )
            return 0

        lax.fori_loop(0, n_op, one_term, 0, unroll=2)

    def send_parts(j, which):
        if relays:
            if which == "other":
                @pl.when(outer)
                def _():
                    relay_copy(j).start()

                part_copy(j, near, z).start()
            else:
                part_copy(j, beside, z).start()
        elif which == "other":
            for i in range(per_half):
                part_copy(j, halves[0] * per_half + i, z).start()
        else:
            for i in range(1, per_half):
                part_copy(j, own_half * per_half + lax.rem(z + i, per_half), z).start()

    def relay(j):
        if not relays:
            return

        @pl.when(jnp.logical_not(outer))
        def _():
            relay_copy(j).wait_recv()
            value = total[j, rows_of(far), :] + relayed[j].astype(jnp.float32)
            zsend[j, rows_of(far), :] = value.astype(jnp.bfloat16)
            part_copy(j, far, z).start()

    def contract(indices, j, first, height, which):
        for index in indices:
            op_peers(lambda peer: left_copy(steps[index], peer, peer).wait_recv())
            op_peers(lambda peer: left_copy(steps[index], peer, o).wait_send())
            send_left(index + AHEAD)
        here = pl.ds(pl.multiple_of(first, height), height)

        def one_state(q, _):
            cols = pl.ds(pl.multiple_of(q * width, width), width)
            value = jnp.dot(
                jnp.concatenate([left[j, a, here, :] for a in range(n_op)], axis=1),
                mixed[j, :, :, cols].reshape(n_op * width, width),
                preferred_element_type=jnp.float32,
            )
            total[j, here, cols] = value
            zsend[j, here, cols] = value.astype(jnp.bfloat16)
            return 0

        lax.fori_loop(0, p_size, one_state, 0, unroll=2)
        for part in which:
            send_parts(j, part)

    def finish(j):
        own = rows_of(z)
        inside = mask_of(j, z * rows, rows)
        if relays:
            part_copy(j, near, near).wait_recv()
            part_copy(j, beside, beside).wait_recv()

            @pl.when(jnp.logical_not(outer))
            def _():
                part_copy(j, far, far).wait_recv()
                total[j, own, :] = total[j, own, :] + zrecv[j, far].astype(jnp.float32)

            peers = [near, beside]
        else:
            sec_peers(lambda peer: part_copy(j, peer, peer).wait_recv())
            peers = [lax.rem(z + i, n_sec) for i in range(1, n_sec)]
        for q in range(p_size):
            cols = pl.ds(q * width, width)
            value = total[j, own, cols]
            for peer in peers:
                value = value + zrecv[j, peer, :, cols].astype(jnp.float32)
            out_ref[j, :, cols] = (value * inside).astype(jnp.bfloat16)

    mix(0)
    last = sectors - 1
    for j in range(sectors):
        if j < last:
            mix(j + 1)
        if j == last:
            for i in range(last - 1):
                finish(i)
        own_copy(j).wait()
        if j < last:
            contract([2 * j, 2 * j + 1], j, 0, width, ["other", "beside"])
            if j > 0:
                relay(j - 1)
        else:
            contract([2 * j], j, halves[0] * tall, tall, ["other"])
            if j > 0:
                relay(j - 1)
            relay(j)
    if relays:
        contract([2 * last + 1], last, beside * rows, rows, ["beside"])
    else:
        contract([2 * last + 1], last, halves[1] * tall, tall, ["beside"])
    if last > 0:
        finish(last - 1)
    if relays:
        contract([2 * last + 2], last, z * rows, rows, [])
    finish(last)

    for j in range(sectors):
        sec_peers(lambda peer: part_copy(j, peer, z).wait_send())


def shards(wave, sector_dims, left_ops, right_ops, site_ops):
    n_op = lax.axis_size("op")
    n_sec = lax.axis_size("sec")
    sectors, width, p_size = wave.shape[0], wave.shape[1], wave.shape[2]
    rows = width // n_sec
    left = left_ops.reshape(n_op, sectors, width, width)
    right = right_ops.reshape(sectors, n_op, width, width)
    sites = jnp.transpose(site_ops, (1, 2, 0))
    wide = p_size * width
    flops = 4 * sectors * n_op * width * width * wide
    sigma = pl.pallas_call(
        functools.partial(kernel, n_op, n_sec),
        out_shape=jax.ShapeDtypeStruct((sectors, rows, wide), jnp.bfloat16),
        in_specs=[
            pl.BlockSpec(memory_space=pltpu.SMEM),
            pl.BlockSpec(memory_space=pltpu.SMEM),
            pl.BlockSpec(memory_space=pl.ANY),
            pl.BlockSpec(memory_space=pl.ANY),
            pl.BlockSpec(memory_space=pl.ANY),
        ],
        out_specs=pl.BlockSpec(memory_space=pltpu.VMEM),
        scratch_shapes=[
            pltpu.VMEM((sectors, width, p_size, width), jnp.bfloat16),
            pltpu.VMEM((sectors, width // CHUNK, p_size, CHUNK, width), jnp.bfloat16),
            pltpu.VMEM((sectors, n_op, width, width), jnp.bfloat16),
            pltpu.VMEM((sectors, n_op, width, width), jnp.bfloat16),
            pltpu.VMEM((sectors, n_op, width, wide), jnp.bfloat16),
            pltpu.VMEM((sectors, width, wide), jnp.float32),
            pltpu.VMEM((sectors, width, wide), jnp.bfloat16),
            pltpu.VMEM((sectors, n_sec, rows, wide), jnp.bfloat16),
            pltpu.VMEM((sectors, rows, wide), jnp.bfloat16),
            pltpu.SemaphoreType.DMA((sectors,)),
            pltpu.SemaphoreType.DMA((sectors,)),
            pltpu.SemaphoreType.DMA((sectors,)),
            pltpu.SemaphoreType.DMA((sectors, 3, n_op)),
            pltpu.SemaphoreType.DMA((sectors, 3, n_op)),
            pltpu.SemaphoreType.DMA((sectors, n_sec)),
            pltpu.SemaphoreType.DMA((sectors, n_sec)),
            pltpu.SemaphoreType.DMA((sectors,)),
        ],
        compiler_params=pltpu.CompilerParams(
            collective_id=0, has_side_effects=True, vmem_limit_bytes=56 * MIB
        ),
        cost_estimate=pl.CostEstimate(flops=flops, bytes_accessed=12 * MIB, transcendentals=0),
    )(sites, sector_dims, wave, left, right)
    return sigma.reshape(sectors, rows, p_size, width)


def solution(mesh):
    placed = (
        P("op", None, None, None),
        P(),
        P(None, ("op", "sec"), None, None),
        P("op", None, "sec", None, None),
        P(),
    )
    return jax.shard_map(
        shards, mesh=mesh, in_specs=placed, out_specs=P("op", "sec", None, None), check_vma=False
    )
```

```python
import functools

import jax
import jax.numpy as jnp
from jax import lax
from jax.experimental import pallas as pl
from jax.experimental.pallas import tpu as pltpu
from jax.sharding import PartitionSpec as P

MESH = pl.DeviceIdType.MESH
MIB = 1024 * 1024
AHEAD = 4
CHUNK = 64


def kernel(
    n_op, n_sec, site_ref, dims_ref, psi_hbm, left_hbm, right_hbm, out_ref,
    psi, right, left, mixed, total, zsend, zrecv, relayed,
    psi_sem, right_sem, lsend_sem, lrecv_sem, zsend_sem, zrecv_sem, relay_sem,
):
    o = lax.axis_index("op")
    z = lax.axis_index("sec")
    sectors, p_size, width = psi.shape[0], psi.shape[1], psi.shape[2]
    rows = width // n_sec
    tall = width // 2
    per_half = n_sec // 2
    relays = n_sec == 4

    own_half = z // per_half
    halves = [1 - own_half, own_half]
    beside = z + 1 - 2 * lax.rem(z, 2)
    far = 3 * halves[0]
    near = 1 + halves[0]
    outer = lax.rem(z, 3) == 0

    def psi_copy(j):
        return pltpu.make_async_copy(psi_hbm.at[j], psi.at[j], psi_sem.at[j])

    def right_copy(j):
        return pltpu.make_async_copy(right_hbm.at[j], right.at[j], right_sem.at[j])

    def rows_of(block):
        return pl.ds(pl.multiple_of(block * rows, rows), rows)

    def rows_in(step):
        return pl.ds(pl.multiple_of(step[2], step[3]), step[3])

    def left_copy(step, peer):
        j, piece = step[:2]
        return pltpu.make_async_remote_copy(
            src_ref=left_hbm.at[peer, j, rows_in(step)],
            dst_ref=left.at[j, o, rows_in(step)],
            send_sem=lsend_sem.at[j, piece], recv_sem=lrecv_sem.at[j, piece],
            device_id=(peer, z), device_id_type=MESH,
        )

    def own_copy(step):
        j, piece = step[:2]
        return pltpu.make_async_copy(
            left_hbm.at[o, j, rows_in(step)], left.at[j, o, rows_in(step)],
            lrecv_sem.at[j, piece],
        )

    def wait_left(step):
        j, piece = step[:2]
        came = left.at[j, :, rows_in(step)]
        pltpu.make_async_copy(came, came, lrecv_sem.at[j, piece]).wait()
        gone = left.at[j, pl.ds(0, n_op - 1), rows_in(step)]
        pltpu.make_async_copy(gone, gone, lsend_sem.at[j, piece]).wait()

    def part_copy(j, peer, slot):
        return pltpu.make_async_remote_copy(
            src_ref=zsend.at[j, rows_of(peer)], dst_ref=zrecv.at[j, slot],
            send_sem=zsend_sem.at[j, peer], recv_sem=zrecv_sem.at[j, slot],
            device_id=(o, peer), device_id_type=MESH,
        )

    def relay_copy(j):
        return pltpu.make_async_remote_copy(
            src_ref=zsend.at[j, rows_of(far)], dst_ref=relayed.at[j],
            send_sem=zsend_sem.at[j, far], recv_sem=relay_sem.at[j],
            device_id=(o, beside), device_id_type=MESH,
        )

    def op_peers(body):
        def step(i, _):
            body(lax.rem(o + i, n_op))
            return 0
        lax.fori_loop(1, n_op, step, 0)

    def sec_peers(body):
        def step(i, _):
            body(lax.rem(z + i, n_sec))
            return 0
        lax.fori_loop(1, n_sec, step, 0)

    steps = []
    for j in range(sectors):
        steps.append((j, 0, halves[0] * tall, tall, "other"))
        if relays and j == sectors - 1:
            steps.append((j, 1, beside * rows, rows, "beside"))
            steps.append((j, 2, z * rows, rows, "none"))
        else:
            steps.append((j, 1, halves[1] * tall, tall, "beside"))

    def send_left(index):
        if index < len(steps):
            op_peers(lambda peer: left_copy(steps[index], peer).start())
            own_copy(steps[index]).start()

    barrier = pltpu.get_barrier_semaphore()
    op_peers(lambda peer: pl.semaphore_signal(
        barrier, inc=1, device_id=(peer, z), device_id_type=MESH))
    sec_peers(lambda peer: pl.semaphore_signal(
        barrier, inc=1, device_id=(o, peer), device_id_type=MESH))
    for j in range(sectors):
        psi_copy(j).start()
        right_copy(j).start()
    pl.semaphore_wait(barrier, n_op + n_sec - 2)

    for index in range(AHEAD):
        send_left(index)

    def mask_of(j, first, height):
        size = dims_ref[o * sectors + j]
        down = lax.broadcasted_iota(jnp.int32, (height, width), 0) + first
        across = lax.broadcasted_iota(jnp.int32, (height, width), 1)
        return jnp.where((down < size) & (across < size), 1.0, 0.0).astype(jnp.float32)

    def mix(j):
        psi_copy(j).wait()
        right_copy(j).wait()
        inside = mask_of(j, 0, width).astype(jnp.bfloat16)
        for p in range(p_size):
            psi[j, p] = psi[j, p] * inside

        def one_term(a, _):
            block = right[j, a]
            term = a * n_sec + z
            weights = [[site_ref[q, p, term] for p in range(p_size)] for q in range(p_size)]
            got = lax.dot_general(
                psi[j].reshape(p_size * width, width), block, (((1,), (1,)), ((), ())),
                preferred_element_type=jnp.float32,
            )
            for c in range(width // CHUNK):
                parts = [
                    got[p * width + c * CHUNK:p * width + (c + 1) * CHUNK] for p in range(p_size)
                ]
                for q in range(p_size):
                    value = weights[q][0] * parts[0]
                    for p in range(1, p_size):
                        value = value + weights[q][p] * parts[p]
                    mixed[j, a, pl.ds(c * CHUNK, CHUNK), pl.ds(q * width, width)] = value.astype(
                        jnp.bfloat16
                    )
            return 0

        lax.fori_loop(0, n_op, one_term, 0)

    def send_parts(j, which):
        if which == "none":
            return
        if relays:
            if which == "other":
                @pl.when(outer)
                def _():
                    relay_copy(j).start()

                part_copy(j, near, z).start()
            else:
                part_copy(j, beside, z).start()
        elif which == "other":
            for i in range(per_half):
                part_copy(j, halves[0] * per_half + i, z).start()
        else:
            for i in range(1, per_half):
                part_copy(j, own_half * per_half + lax.rem(z + i, per_half), z).start()

    def relay(j):
        if not relays:
            return

        @pl.when(jnp.logical_not(outer))
        def _():
            relay_copy(j).wait_recv()
            value = total[j, rows_of(far), :] + relayed[j].astype(jnp.float32)
            zsend[j, rows_of(far), :] = value.astype(jnp.bfloat16)
            part_copy(j, far, z).start()

    def contract(index):
        step = steps[index]
        j, which = step[0], step[4]
        wait_left(step)
        send_left(index + AHEAD)
        here = rows_in(step)

        def one_state(q, _):
            cols = pl.ds(pl.multiple_of(q * width, width), width)
            value = jnp.dot(
                jnp.concatenate([left[j, a, here, :] for a in range(n_op)], axis=1),
                mixed[j, :, :, cols].reshape(n_op * width, width),
                preferred_element_type=jnp.float32,
            )
            total[j, here, cols] = value
            zsend[j, here, cols] = value.astype(jnp.bfloat16)
            return 0

        lax.fori_loop(0, p_size, one_state, 0)
        send_parts(j, which)

    def finish(j):
        own = rows_of(z)
        inside = mask_of(j, z * rows, rows)
        if relays:
            part_copy(j, near, near).wait_recv()
            part_copy(j, beside, beside).wait_recv()

            @pl.when(jnp.logical_not(outer))
            def _():
                part_copy(j, far, far).wait_recv()
                total[j, own, :] = total[j, own, :] + zrecv[j, far].astype(jnp.float32)

            peers = [near, beside]
        else:
            sec_peers(lambda peer: part_copy(j, peer, peer).wait_recv())
            peers = [lax.rem(z + i, n_sec) for i in range(1, n_sec)]
        for q in range(p_size):
            cols = pl.ds(q * width, width)
            value = total[j, own, cols]
            for peer in peers:
                value = value + zrecv[j, peer, :, cols].astype(jnp.float32)
            out_ref[j, :, cols] = (value * inside).astype(jnp.bfloat16)

    mix(0)
    last = sectors - 1
    for j in range(sectors):
        if j < last:
            mix(j + 1)
        if j == last:
            for i in range(last - 1):
                finish(i)
        contract(2 * j)
        if j > 0:
            relay(j - 1)
        if j == last:
            relay(j)
        contract(2 * j + 1)
    if last > 0:
        finish(last - 1)
    if relays:
        contract(2 * sectors)
    finish(last)

    for j in range(sectors):
        sec_peers(lambda peer: part_copy(j, peer, z).wait_send())


def shards(wave, sector_dims, left_ops, right_ops, site_ops):
    n_op = lax.axis_size("op")
    n_sec = lax.axis_size("sec")
    sectors, width, p_size = wave.shape[0], wave.shape[1], wave.shape[2]
    rows = width // n_sec
    left = left_ops.reshape(n_op, sectors, width, width)
    right = right_ops.reshape(sectors, n_op, width, width)
    sites = jnp.transpose(site_ops, (1, 2, 0))
    wide = p_size * width
    flops = 4 * sectors * n_op * width * width * wide
    waves = jnp.transpose(wave, (0, 2, 1, 3))
    sigma = pl.pallas_call(
        functools.partial(kernel, n_op, n_sec),
        out_shape=jax.ShapeDtypeStruct((sectors, rows, wide), jnp.bfloat16),
        in_specs=[
            pl.BlockSpec(memory_space=pltpu.SMEM),
            pl.BlockSpec(memory_space=pltpu.SMEM),
            pl.BlockSpec(memory_space=pl.ANY),
            pl.BlockSpec(memory_space=pl.ANY),
            pl.BlockSpec(memory_space=pl.ANY),
        ],
        out_specs=pl.BlockSpec(memory_space=pltpu.VMEM),
        scratch_shapes=[
            pltpu.VMEM((sectors, p_size, width, width), jnp.bfloat16),
            pltpu.VMEM((sectors, n_op, width, width), jnp.bfloat16),
            pltpu.VMEM((sectors, n_op, width, width), jnp.bfloat16),
            pltpu.VMEM((sectors, n_op, width, wide), jnp.bfloat16),
            pltpu.VMEM((sectors, width, wide), jnp.float32),
            pltpu.VMEM((sectors, width, wide), jnp.bfloat16),
            pltpu.VMEM((sectors, n_sec, rows, wide), jnp.bfloat16),
            pltpu.VMEM((sectors, rows, wide), jnp.bfloat16),
            pltpu.SemaphoreType.DMA((sectors,)),
            pltpu.SemaphoreType.DMA((sectors,)),
            pltpu.SemaphoreType.DMA((sectors, 3)),
            pltpu.SemaphoreType.DMA((sectors, 3)),
            pltpu.SemaphoreType.DMA((sectors, n_sec)),
            pltpu.SemaphoreType.DMA((sectors, n_sec)),
            pltpu.SemaphoreType.DMA((sectors,)),
        ],
        compiler_params=pltpu.CompilerParams(
            collective_id=0, has_side_effects=True, vmem_limit_bytes=48 * MIB
        ),
        cost_estimate=pl.CostEstimate(flops=flops, bytes_accessed=12 * MIB, transcendentals=0),
    )(sites, sector_dims, waves, left, right)
    return sigma.reshape(sectors, rows, p_size, width)


def solution(mesh):
    placed = (
        P("op", None, None, None),
        P(),
        P(None, ("op", "sec"), None, None),
        P("op", None, "sec", None, None),
        P(),
    )
    return jax.shard_map(
        shards, mesh=mesh, in_specs=placed, out_specs=P("op", "sec", None, None), check_vma=False
    )
```

```python
import functools

import jax
import jax.numpy as jnp
from jax import lax
from jax.experimental import pallas as pl
from jax.experimental.pallas import tpu as pltpu
from jax.sharding import PartitionSpec as P

MESH = pl.DeviceIdType.MESH
MIB = 1024 * 1024
AHEAD = 4
CHUNK = 16


def kernel(
    n_op, n_sec, site_ref, dims_ref, psi_hbm, left_hbm, right_hbm, out_ref,
    psi, right, left, mixed, total, zsend, zrecv, relayed, turned,
    psi_sem, right_sem, lsend_sem, lrecv_sem, zsend_sem, zrecv_sem, relay_sem,
):
    o = lax.axis_index("op")
    z = lax.axis_index("sec")
    sectors, p_size, width = psi.shape[0], psi.shape[1], psi.shape[2]
    rows = width // n_sec
    tall = width // 2
    per_half = n_sec // 2
    relays = n_sec == 4

    own_half = z // per_half
    halves = [1 - own_half, own_half]
    beside = z + 1 - 2 * lax.rem(z, 2)
    far = 3 * halves[0]
    near = 1 + halves[0]
    outer = lax.rem(z, 3) == 0

    def psi_copy(j):
        return pltpu.make_async_copy(psi_hbm.at[j], psi.at[j], psi_sem.at[j])

    def right_copy(j):
        return pltpu.make_async_copy(right_hbm.at[j], right.at[j], right_sem.at[j])

    def rows_of(block):
        return pl.ds(pl.multiple_of(block * rows, rows), rows)

    def rows_in(step):
        return pl.ds(pl.multiple_of(step[2], step[3]), step[3])

    def left_copy(step, peer):
        j, piece = step[:2]
        return pltpu.make_async_remote_copy(
            src_ref=left_hbm.at[peer, j, rows_in(step)],
            dst_ref=left.at[j, o, rows_in(step)],
            send_sem=lsend_sem.at[j, piece], recv_sem=lrecv_sem.at[j, piece],
            device_id=(peer, z), device_id_type=MESH,
        )

    def own_copy(step):
        j, piece = step[:2]
        return pltpu.make_async_copy(
            left_hbm.at[o, j, rows_in(step)], left.at[j, o, rows_in(step)],
            lrecv_sem.at[j, piece],
        )

    def wait_left(step):
        j, piece = step[:2]
        came = left.at[j, :, rows_in(step)]
        pltpu.make_async_copy(came, came, lrecv_sem.at[j, piece]).wait()
        gone = left.at[j, pl.ds(0, n_op - 1), rows_in(step)]
        pltpu.make_async_copy(gone, gone, lsend_sem.at[j, piece]).wait()

    def part_copy(j, peer, slot):
        return pltpu.make_async_remote_copy(
            src_ref=zsend.at[j, rows_of(peer)], dst_ref=zrecv.at[j, slot],
            send_sem=zsend_sem.at[j, peer], recv_sem=zrecv_sem.at[j, slot],
            device_id=(o, peer), device_id_type=MESH,
        )

    def relay_copy(j):
        return pltpu.make_async_remote_copy(
            src_ref=zsend.at[j, rows_of(far)], dst_ref=relayed.at[j],
            send_sem=zsend_sem.at[j, far], recv_sem=relay_sem.at[j],
            device_id=(o, beside), device_id_type=MESH,
        )

    def op_peers(body):
        def step(i, _):
            body(lax.rem(o + i, n_op))
            return 0
        lax.fori_loop(1, n_op, step, 0)

    def sec_peers(body):
        def step(i, _):
            body(lax.rem(z + i, n_sec))
            return 0
        lax.fori_loop(1, n_sec, step, 0)

    steps = []
    for j in range(sectors):
        steps.append((j, 0, halves[0] * tall, tall, "other"))
        if relays and j == sectors - 1:
            steps.append((j, 1, beside * rows, rows, "beside"))
            steps.append((j, 2, z * rows, rows, "none"))
        else:
            steps.append((j, 1, halves[1] * tall, tall, "beside"))

    def send_left(index):
        if index < len(steps):
            op_peers(lambda peer: left_copy(steps[index], peer).start())
            own_copy(steps[index]).start()

    barrier = pltpu.get_barrier_semaphore()
    op_peers(lambda peer: pl.semaphore_signal(
        barrier, inc=1, device_id=(peer, z), device_id_type=MESH))
    sec_peers(lambda peer: pl.semaphore_signal(
        barrier, inc=1, device_id=(o, peer), device_id_type=MESH))
    for j in range(sectors):
        psi_copy(j).start()
        right_copy(j).start()
    pl.semaphore_wait(barrier, n_op + n_sec - 2)

    for index in range(AHEAD):
        send_left(index)

    def mask_of(j, first, height):
        size = dims_ref[o * sectors + j]
        down = lax.broadcasted_iota(jnp.int32, (height, width), 0) + first
        across = lax.broadcasted_iota(jnp.int32, (height, width), 1)
        return jnp.where((down < size) & (across < size), 1.0, 0.0).astype(jnp.float32)

    def mix(j):
        psi_copy(j).wait()
        right_copy(j).wait()
        inside = mask_of(j, 0, width).astype(jnp.bfloat16)
        for p in range(p_size):
            psi[j, p] = psi[j, p] * inside

        def right_dot(a, slot):
            turned[slot] = lax.dot_general(
                psi[j].reshape(p_size * width, width), right[j, a], (((1,), (1,)), ((), ())),
                preferred_element_type=jnp.float32,
            )

        def site_mix(a, slot):
            term = a * n_sec + z
            weights = [[site_ref[q, p, term] for p in range(p_size)] for q in range(p_size)]
            for c in range(width // CHUNK):
                here = pl.ds(c * CHUNK, CHUNK)
                parts = [
                    turned[slot, pl.ds(p * width + c * CHUNK, CHUNK), :] for p in range(p_size)
                ]
                for q in range(p_size):
                    value = weights[q][0] * parts[0]
                    for p in range(1, p_size):
                        value = value + weights[q][p] * parts[p]
                    mixed[j, a, here, pl.ds(q * width, width)] = value.astype(jnp.bfloat16)

        def two_terms(i, _):
            a = 2 * i
            right_dot(a + 1, 1)
            site_mix(a, 0)
            right_dot(lax.rem(a + 2, n_op), 0)
            site_mix(a + 1, 1)
            return 0

        right_dot(0, 0)
        lax.fori_loop(0, n_op // 2, two_terms, 0)

    def send_parts(j, which):
        if which == "none":
            return
        if relays:
            if which == "other":
                @pl.when(outer)
                def _():
                    relay_copy(j).start()

                part_copy(j, near, z).start()
            else:
                part_copy(j, beside, z).start()
        elif which == "other":
            for i in range(per_half):
                part_copy(j, halves[0] * per_half + i, z).start()
        else:
            for i in range(1, per_half):
                part_copy(j, own_half * per_half + lax.rem(z + i, per_half), z).start()

    def relay(j):
        if not relays:
            return

        @pl.when(jnp.logical_not(outer))
        def _():
            relay_copy(j).wait_recv()
            value = total[j, rows_of(far), :] + relayed[j].astype(jnp.float32)
            zsend[j, rows_of(far), :] = value.astype(jnp.bfloat16)
            part_copy(j, far, z).start()

    def contract(index):
        step = steps[index]
        j, which = step[0], step[4]
        wait_left(step)
        send_left(index + AHEAD)
        here = rows_in(step)

        def one_state(q, _):
            cols = pl.ds(pl.multiple_of(q * width, width), width)
            value = jnp.dot(
                jnp.concatenate([left[j, a, here, :] for a in range(n_op)], axis=1),
                mixed[j, :, :, cols].reshape(n_op * width, width),
                preferred_element_type=jnp.float32,
            )
            total[j, here, cols] = value
            zsend[j, here, cols] = value.astype(jnp.bfloat16)
            return 0

        lax.fori_loop(0, p_size, one_state, 0)
        send_parts(j, which)

    def finish(j):
        own = rows_of(z)
        inside = mask_of(j, z * rows, rows)
        if relays:
            part_copy(j, near, near).wait_recv()
            part_copy(j, beside, beside).wait_recv()

            @pl.when(jnp.logical_not(outer))
            def _():
                part_copy(j, far, far).wait_recv()
                total[j, own, :] = total[j, own, :] + zrecv[j, far].astype(jnp.float32)

            peers = [near, beside]
        else:
            sec_peers(lambda peer: part_copy(j, peer, peer).wait_recv())
            peers = [lax.rem(z + i, n_sec) for i in range(1, n_sec)]
        for q in range(p_size):
            cols = pl.ds(q * width, width)
            value = total[j, own, cols]
            for peer in peers:
                value = value + zrecv[j, peer, :, cols].astype(jnp.float32)
            out_ref[j, :, cols] = (value * inside).astype(jnp.bfloat16)

    mix(0)
    last = sectors - 1
    for j in range(sectors):
        if j < last:
            mix(j + 1)
        if j == last:
            for i in range(last - 1):
                finish(i)
        contract(2 * j)
        if j > 0:
            relay(j - 1)
        if j == last:
            relay(j)
        contract(2 * j + 1)
    if last > 0:
        finish(last - 1)
    if relays:
        contract(2 * sectors)
    finish(last)

    for j in range(sectors):
        sec_peers(lambda peer: part_copy(j, peer, z).wait_send())


def shards(wave, sector_dims, left_ops, right_ops, site_ops):
    n_op = lax.axis_size("op")
    n_sec = lax.axis_size("sec")
    sectors, width, p_size = wave.shape[0], wave.shape[1], wave.shape[2]
    rows = width // n_sec
    left = left_ops.reshape(n_op, sectors, width, width)
    right = right_ops.reshape(sectors, n_op, width, width)
    sites = jnp.transpose(site_ops, (1, 2, 0))
    wide = p_size * width
    flops = 4 * sectors * n_op * width * width * wide
    waves = jnp.transpose(wave, (0, 2, 1, 3))
    sigma = pl.pallas_call(
        functools.partial(kernel, n_op, n_sec),
        out_shape=jax.ShapeDtypeStruct((sectors, rows, wide), jnp.bfloat16),
        in_specs=[
            pl.BlockSpec(memory_space=pltpu.SMEM),
            pl.BlockSpec(memory_space=pltpu.SMEM),
            pl.BlockSpec(memory_space=pl.ANY),
            pl.BlockSpec(memory_space=pl.ANY),
            pl.BlockSpec(memory_space=pl.ANY),
        ],
        out_specs=pl.BlockSpec(memory_space=pltpu.VMEM),
        scratch_shapes=[
            pltpu.VMEM((sectors, p_size, width, width), jnp.bfloat16),
            pltpu.VMEM((sectors, n_op, width, width), jnp.bfloat16),
            pltpu.VMEM((sectors, n_op, width, width), jnp.bfloat16),
            pltpu.VMEM((sectors, n_op, width, wide), jnp.bfloat16),
            pltpu.VMEM((sectors, width, wide), jnp.float32),
            pltpu.VMEM((sectors, width, wide), jnp.bfloat16),
            pltpu.VMEM((sectors, n_sec, rows, wide), jnp.bfloat16),
            pltpu.VMEM((sectors, rows, wide), jnp.bfloat16),
            pltpu.VMEM((2, wide, width), jnp.float32),
            pltpu.SemaphoreType.DMA((sectors,)),
            pltpu.SemaphoreType.DMA((sectors,)),
            pltpu.SemaphoreType.DMA((sectors, 3)),
            pltpu.SemaphoreType.DMA((sectors, 3)),
            pltpu.SemaphoreType.DMA((sectors, n_sec)),
            pltpu.SemaphoreType.DMA((sectors, n_sec)),
            pltpu.SemaphoreType.DMA((sectors,)),
        ],
        compiler_params=pltpu.CompilerParams(
            collective_id=0, has_side_effects=True, vmem_limit_bytes=48 * MIB
        ),
        cost_estimate=pl.CostEstimate(flops=flops, bytes_accessed=12 * MIB, transcendentals=0),
    )(sites, sector_dims, waves, left, right)
    return sigma.reshape(sectors, rows, p_size, width)


def solution(mesh):
    placed = (
        P("op", None, None, None),
        P(),
        P(None, ("op", "sec"), None, None),
        P("op", None, "sec", None, None),
        P(),
    )
    return jax.shard_map(
        shards, mesh=mesh, in_specs=placed, out_specs=P("op", "sec", None, None), check_vma=False
    )
```

```python
import functools

import jax
import jax.numpy as jnp
from jax import lax
from jax.experimental import pallas as pl
from jax.experimental.pallas import tpu as pltpu
from jax.sharding import PartitionSpec as P

MESH = pl.DeviceIdType.MESH
MIB = 1024 * 1024
AHEAD = 6
CHUNK = 16


def kernel(
    n_op, n_sec, site_ref, dims_ref, psi_hbm, left_hbm, right_hbm, out_ref,
    psi, right, left, mixed, total, zsend, zrecv, relayed, turned,
    psi_sem, right_sem, lsend_sem, lrecv_sem, zsend_sem, zrecv_sem, relay_sem,
):
    o = lax.axis_index("op")
    z = lax.axis_index("sec")
    sectors, p_size, width = psi.shape[0], psi.shape[1], psi.shape[2]
    rows = width // n_sec
    tall = width // 2
    per_half = n_sec // 2
    relays = n_sec == 4

    own_half = z // per_half
    halves = [1 - own_half, own_half]
    beside = z + 1 - 2 * lax.rem(z, 2)
    far = 3 * halves[0]
    near = 1 + halves[0]
    outer = lax.rem(z, 3) == 0

    def psi_copy(j):
        return pltpu.make_async_copy(psi_hbm.at[j], psi.at[j], psi_sem.at[j])

    def right_copy(j):
        return pltpu.make_async_copy(right_hbm.at[j], right.at[j], right_sem.at[j])

    def rows_of(block):
        return pl.ds(pl.multiple_of(block * rows, rows), rows)

    def rows_in(step):
        return pl.ds(pl.multiple_of(step[2], step[3]), step[3])

    def left_copy(step, peer):
        j, piece = step[:2]
        return pltpu.make_async_remote_copy(
            src_ref=left_hbm.at[peer, j, rows_in(step)],
            dst_ref=left.at[j, o, rows_in(step)],
            send_sem=lsend_sem.at[j, piece], recv_sem=lrecv_sem.at[j, piece],
            device_id=(peer, z), device_id_type=MESH,
        )

    def own_copy(step):
        j, piece = step[:2]
        return pltpu.make_async_copy(
            left_hbm.at[o, j, rows_in(step)], left.at[j, o, rows_in(step)],
            lrecv_sem.at[j, piece],
        )

    def wait_left(step):
        j, piece = step[:2]
        came = left.at[j, :, rows_in(step)]
        pltpu.make_async_copy(came, came, lrecv_sem.at[j, piece]).wait()
        gone = left.at[j, pl.ds(0, n_op - 1), rows_in(step)]
        pltpu.make_async_copy(gone, gone, lsend_sem.at[j, piece]).wait()

    def part_copy(j, peer, slot):
        return pltpu.make_async_remote_copy(
            src_ref=zsend.at[j, rows_of(peer)], dst_ref=zrecv.at[j, slot],
            send_sem=zsend_sem.at[j, peer], recv_sem=zrecv_sem.at[j, slot],
            device_id=(o, peer), device_id_type=MESH,
        )

    def relay_copy(j):
        return pltpu.make_async_remote_copy(
            src_ref=zsend.at[j, rows_of(far)], dst_ref=relayed.at[j],
            send_sem=zsend_sem.at[j, far], recv_sem=relay_sem.at[j],
            device_id=(o, beside), device_id_type=MESH,
        )

    def op_peers(body):
        def step(i, _):
            body(lax.rem(o + i, n_op))
            return 0
        lax.fori_loop(1, n_op, step, 0)

    def sec_peers(body):
        def step(i, _):
            body(lax.rem(z + i, n_sec))
            return 0
        lax.fori_loop(1, n_sec, step, 0)

    steps = []
    for j in range(sectors):
        steps.append((j, 0, halves[0] * tall, tall, "other"))
        if relays and j == sectors - 1:
            steps.append((j, 1, beside * rows, rows, "beside"))
            steps.append((j, 2, z * rows, rows, "none"))
        else:
            steps.append((j, 1, halves[1] * tall, tall, "beside"))

    def send_left(index):
        if index < len(steps):
            op_peers(lambda peer: left_copy(steps[index], peer).start())
            own_copy(steps[index]).start()

    barrier = pltpu.get_barrier_semaphore()
    op_peers(lambda peer: pl.semaphore_signal(
        barrier, inc=1, device_id=(peer, z), device_id_type=MESH))
    sec_peers(lambda peer: pl.semaphore_signal(
        barrier, inc=1, device_id=(o, peer), device_id_type=MESH))
    for j in range(sectors):
        psi_copy(j).start()
        right_copy(j).start()
    pl.semaphore_wait(barrier, n_op + n_sec - 2)

    for index in range(AHEAD):
        send_left(index)

    def mask_of(j, first, height):
        size = dims_ref[o * sectors + j]
        down = lax.broadcasted_iota(jnp.int32, (height, width), 0) + first
        across = lax.broadcasted_iota(jnp.int32, (height, width), 1)
        return jnp.where((down < size) & (across < size), 1.0, 0.0).astype(jnp.float32)

    def mix(j):
        psi_copy(j).wait()
        right_copy(j).wait()
        inside = mask_of(j, 0, width).astype(jnp.bfloat16)
        for p in range(p_size):
            psi[j, p] = psi[j, p] * inside

        def right_dot(a, slot):
            turned[slot] = lax.dot_general(
                psi[j].reshape(p_size * width, width), right[j, a], (((1,), (1,)), ((), ())),
                preferred_element_type=jnp.float32,
            )

        def site_mix(a, slot):
            term = a * n_sec + z
            weights = [[site_ref[q, p, term] for p in range(p_size)] for q in range(p_size)]
            for c in range(width // CHUNK):
                here = pl.ds(c * CHUNK, CHUNK)
                parts = [
                    turned[slot, pl.ds(p * width + c * CHUNK, CHUNK), :] for p in range(p_size)
                ]
                for q in range(p_size):
                    value = weights[q][0] * parts[0]
                    for p in range(1, p_size):
                        value = value + weights[q][p] * parts[p]
                    mixed[j, a, here, pl.ds(q * width, width)] = value.astype(jnp.bfloat16)

        def two_terms(i, _):
            a = 2 * i
            right_dot(a + 1, 1)
            site_mix(a, 0)
            right_dot(lax.rem(a + 2, n_op), 0)
            site_mix(a + 1, 1)
            return 0

        right_dot(0, 0)
        lax.fori_loop(0, n_op // 2, two_terms, 0)

    def send_parts(j, which):
        if which == "none":
            return
        if relays:
            if which == "other":
                @pl.when(outer)
                def _():
                    relay_copy(j).start()

                part_copy(j, near, z).start()
            else:
                part_copy(j, beside, z).start()
        elif which == "other":
            for i in range(per_half):
                part_copy(j, halves[0] * per_half + i, z).start()
        else:
            for i in range(1, per_half):
                part_copy(j, own_half * per_half + lax.rem(z + i, per_half), z).start()

    def relay(j):
        if not relays:
            return

        @pl.when(jnp.logical_not(outer))
        def _():
            relay_copy(j).wait_recv()
            value = total[j, rows_of(far), :] + relayed[j].astype(jnp.float32)
            zsend[j, rows_of(far), :] = value.astype(jnp.bfloat16)
            part_copy(j, far, z).start()

    def contract(index):
        step = steps[index]
        j, which = step[0], step[4]
        wait_left(step)
        send_left(index + AHEAD)
        here = rows_in(step)

        def one_state(q, _):
            cols = pl.ds(pl.multiple_of(q * width, width), width)
            value = jnp.dot(
                jnp.concatenate([left[j, a, here, :] for a in range(n_op)], axis=1),
                mixed[j, :, :, cols].reshape(n_op * width, width),
                preferred_element_type=jnp.float32,
            )
            total[j, here, cols] = value
            zsend[j, here, cols] = value.astype(jnp.bfloat16)
            return 0

        lax.fori_loop(0, p_size, one_state, 0)
        send_parts(j, which)

    def finish(j):
        own = rows_of(z)
        inside = mask_of(j, z * rows, rows)
        if relays:
            part_copy(j, near, near).wait_recv()
            part_copy(j, beside, beside).wait_recv()

            @pl.when(jnp.logical_not(outer))
            def _():
                part_copy(j, far, far).wait_recv()
                total[j, own, :] = total[j, own, :] + zrecv[j, far].astype(jnp.float32)

            peers = [near, beside]
        else:
            sec_peers(lambda peer: part_copy(j, peer, peer).wait_recv())
            peers = [lax.rem(z + i, n_sec) for i in range(1, n_sec)]
        for q in range(p_size):
            cols = pl.ds(q * width, width)
            value = total[j, own, cols]
            for peer in peers:
                value = value + zrecv[j, peer, :, cols].astype(jnp.float32)
            out_ref[j, :, cols] = (value * inside).astype(jnp.bfloat16)

    mix(0)
    last = sectors - 1
    for j in range(sectors):
        if j < last:
            mix(j + 1)
        if j == last:
            for i in range(last - 1):
                finish(i)
        contract(2 * j)
        if j > 0:
            relay(j - 1)
        if j == last:
            relay(j)
        contract(2 * j + 1)
    if last > 0:
        finish(last - 1)
    if relays:
        contract(2 * sectors)
    finish(last)

    for j in range(sectors):
        sec_peers(lambda peer: part_copy(j, peer, z).wait_send())


def shards(wave, sector_dims, left_ops, right_ops, site_ops):
    n_op = lax.axis_size("op")
    n_sec = lax.axis_size("sec")
    sectors, width, p_size = wave.shape[0], wave.shape[1], wave.shape[2]
    rows = width // n_sec
    left = left_ops.reshape(n_op, sectors, width, width)
    right = right_ops.reshape(sectors, n_op, width, width)
    sites = jnp.transpose(site_ops, (1, 2, 0))
    wide = p_size * width
    flops = 4 * sectors * n_op * width * width * wide
    waves = jnp.transpose(wave, (0, 2, 1, 3))
    sigma = pl.pallas_call(
        functools.partial(kernel, n_op, n_sec),
        out_shape=jax.ShapeDtypeStruct((sectors, rows, wide), jnp.bfloat16),
        in_specs=[
            pl.BlockSpec(memory_space=pltpu.SMEM),
            pl.BlockSpec(memory_space=pltpu.SMEM),
            pl.BlockSpec(memory_space=pl.ANY),
            pl.BlockSpec(memory_space=pl.ANY),
            pl.BlockSpec(memory_space=pl.ANY),
        ],
        out_specs=pl.BlockSpec(memory_space=pltpu.VMEM),
        scratch_shapes=[
            pltpu.VMEM((sectors, p_size, width, width), jnp.bfloat16),
            pltpu.VMEM((sectors, n_op, width, width), jnp.bfloat16),
            pltpu.VMEM((sectors, n_op, width, width), jnp.bfloat16),
            pltpu.VMEM((sectors, n_op, width, wide), jnp.bfloat16),
            pltpu.VMEM((sectors, width, wide), jnp.float32),
            pltpu.VMEM((sectors, width, wide), jnp.bfloat16),
            pltpu.VMEM((sectors, n_sec, rows, wide), jnp.bfloat16),
            pltpu.VMEM((sectors, rows, wide), jnp.bfloat16),
            pltpu.VMEM((2, wide, width), jnp.float32),
            pltpu.SemaphoreType.DMA((sectors,)),
            pltpu.SemaphoreType.DMA((sectors,)),
            pltpu.SemaphoreType.DMA((sectors, 3)),
            pltpu.SemaphoreType.DMA((sectors, 3)),
            pltpu.SemaphoreType.DMA((sectors, n_sec)),
            pltpu.SemaphoreType.DMA((sectors, n_sec)),
            pltpu.SemaphoreType.DMA((sectors,)),
        ],
        compiler_params=pltpu.CompilerParams(
            collective_id=0, has_side_effects=True, vmem_limit_bytes=48 * MIB
        ),
        cost_estimate=pl.CostEstimate(flops=flops, bytes_accessed=12 * MIB, transcendentals=0),
    )(sites, sector_dims, waves, left, right)
    return sigma.reshape(sectors, rows, p_size, width)


def solution(mesh):
    placed = (
        P("op", None, None, None),
        P(),
        P(None, ("op", "sec"), None, None),
        P("op", None, "sec", None, None),
        P(),
    )
    return jax.shard_map(
        shards, mesh=mesh, in_specs=placed, out_specs=P("op", "sec", None, None), check_vma=False
    )
```
